32 devices in a mesh: ctx: 16 (over z, x, core), grp: 2 (over y).
Axes of the slice: x: 2, y: 2, z: 4, core: 2. Of those that a mesh axis runs over, the one named last changes fastest.
Arguments:
- inputs_se: bfloat16 [3, 2048, 8192], P(None, 'ctx', 'grp'), may hold values from -6 to 6
- cotangent_se: bfloat16 [2048, 8192], P('ctx', 'grp'), may hold values from -6 to 6
- kernel_se: bfloat16 [512, 7], P('grp'), may hold values from -2 to 2
- skip_se: float32 [8192], P('grp'), may hold values from -4 to 4
- inputs_mr: bfloat16 [3, 2048, 8192], P(None, 'ctx', 'grp'), may hold values from -6 to 6
- kernel_mr: bfloat16 [512, 128], P('grp'), may hold values from -0.5 to 0.5
- skip_mr: float32 [8192], P('grp'), may hold values from -4 to 4
- out_weight: bfloat16 [8192, 4096], P('grp', 'ctx'), may hold values from -0.0625 to 0.0625
- cotangent_out: bfloat16 [2048, 4096], P('ctx', 'grp'), may hold values from -6 to 6
Outputs:
- mixed_se: bfloat16 [2048, 8192], P('ctx', 'grp')
- projected: bfloat16 [2048, 4096], P('ctx', 'grp')
- grad_inputs_se: bfloat16 [3, 2048, 8192], P(None, 'ctx', 'grp')
- grad_inputs_mr: bfloat16 [3, 2048, 8192], P(None, 'ctx', 'grp')
- grad_kernel_se: float32 [512, 7], P('grp')
- grad_kernel_mr: float32 [512, 128], P('grp')
- grad_skip_se: float32 [8192], P('grp')
- grad_skip_mr: float32 [8192], P('grp')
- grad_out_weight: float32 [8192, 4096], P('grp', 'ctx')
The draws below stay inside these ranges and needn't reach their ends.
All inputs are finite; a program needn't handle non-finite values.
Results may differ from the reference program's by a relative error of at most 0.012.
Values may be sent and summed in bfloat16 or wider, within the bound.
A program may use at most 256 MiB of HBM per device.

```python
import jax
import jax.numpy as jnp
from jax import lax

D = 8192
OUT_W = 4096
SE_LEN = 7
MR_LEN = 128
TOK_DEV = 128
S = 2048
G = 512
N_CTX = 16


def raised(array, stream_key, source, target, blocks, factor):
    owner, partner = [(jnp.arange(array.shape[axis_at]) // (array.shape[axis_at] // blocks)).reshape([-1 if axis == axis_at else 1 for axis in range(array.ndim)]) for axis_at in (source, target)]
    chosen = jax.random.permutation(stream_key, blocks)[partner]
    strong = (owner == chosen) | (owner == (partner + blocks // 2) % blocks)
    return jnp.where(strong, factor * array, array)


def steps_of(rng, dims, shards, least, high):
    def one(axis_at, shards_of):
        heights = jax.random.uniform(jax.random.fold_in(jax.random.fold_in(rng, 6), axis_at), (shards_of,), jnp.float32, least / len(shards), high / len(shards))
        return jnp.repeat(jnp.exp(heights), dims[axis_at] // shards_of).reshape((-1,) + (1,) * (len(dims) - axis_at - 1))

    level = one(*shards[0])
    for cut in shards[1:]:
        level = level * one(*cut)
    return level


def bell_draw(rng, extent, deviation, bound, split=(), kind=jnp.bfloat16):
    drawn = deviation * jax.random.normal(rng, extent, jnp.float32)
    if split:
        drawn = drawn * steps_of(rng, extent, split, -0.22, 0.18)
    return jnp.clip(drawn, -bound, bound).astype(kind)


def gaussian_with(rng, shape, width, reach, split, heavy, held_as=jnp.bfloat16):
    array = width * jax.random.normal(rng, shape, jnp.float32)
    if split:
        array = array * steps_of(rng, shape, split, -0.22, 0.18)
    return jnp.clip(raised(array, jax.random.fold_in(rng, 3), *heavy), -reach, reach).astype(held_as)


def setup_inputs(seed: int = 0) -> dict:
    key_list = jax.random.split(jax.random.key(seed), 10)
    inputs_se = bell_draw(key_list[0], (3, S, D), 1.0, 6.0, ((1, 16), (2, 2)))
    cotangent_se = bell_draw(key_list[1], (S, D), 1.0, 6.0, ((0, 16), (1, 2)))
    kernel_se = bell_draw(key_list[2], (G, SE_LEN), SE_LEN ** -0.5, 2.0, ((0, 2),))
    skip_se = bell_draw(key_list[3], (D,), 1.0, 4.0, ((0, 2),), jnp.float32)
    inputs_mr = bell_draw(key_list[4], (3, S, D), 1.0, 6.0, ((1, 16), (2, 2)))
    kernel_mr = bell_draw(key_list[5], (G, MR_LEN), MR_LEN ** -0.5, 0.5, ((0, 2),))
    skip_mr = bell_draw(key_list[6], (D,), 1.0, 4.0, ((0, 2),), jnp.float32)
    out_weight = bell_draw(key_list[7], (D, OUT_W), D ** -0.5, 0.0625, ((0, 2), (1, 16)))
    cotangent_out = gaussian_with(key_list[8], (S, OUT_W), 1.0, 6.0, ((0, 16), (1, 2)), (0, 1, 16, 2.0))
    return dict(inputs_se=inputs_se, cotangent_se=cotangent_se, kernel_se=kernel_se, skip_se=skip_se, inputs_mr=inputs_mr, kernel_mr=kernel_mr, skip_mr=skip_mr, out_weight=out_weight, cotangent_out=cotangent_out)


HIGH = lax.Precision.HIGHEST


def band_tables(length, tile_rows):
    row_ids = jnp.arange(tile_rows, dtype=jnp.int32)[:, None, None]
    col_ids = jnp.arange(tile_rows, dtype=jnp.int32)[None, :, None]
    tap_ids = jnp.arange(length, dtype=jnp.int32)[None, None, :]
    inside = (row_ids - col_ids == tap_ids).astype(jnp.float32)
    across = (row_ids - col_ids + tile_rows == tap_ids).astype(jnp.float32)
    return inside, across


def layer_forward(inputs, kernel, skip_scale):
    query_in = inputs[0].astype(jnp.float32)
    key_in = inputs[1].astype(jnp.float32)
    value_in = inputs[2].astype(jnp.float32)
    product_low = (key_in * value_in).astype(jnp.bfloat16)
    product = lax.optimization_barrier(product_low).astype(jnp.float32)
    tile_rows = MR_LEN
    row_count, channels = product.shape
    groups = kernel.shape[0]
    tiled = product.reshape(row_count // tile_rows, tile_rows, groups, channels // groups)
    earlier = jnp.concatenate([jnp.zeros_like(tiled[:1]), tiled[:-1]], 0)
    inside, across = band_tables(kernel.shape[1], tile_rows)
    taps_f = kernel.astype(jnp.float32)
    near_band = jnp.einsum("gs,ijs->gij", taps_f, inside, precision=HIGH)
    far_band = jnp.einsum("gs,ijs->gij", taps_f, across, precision=HIGH)
    convolved = jnp.einsum("gij,njgc->nigc", near_band, tiled, precision=HIGH)
    convolved = convolved + jnp.einsum("gij,njgc->nigc", far_band, earlier, precision=HIGH)
    convolved = convolved.reshape(row_count, channels) + skip_scale * product
    mixed = (query_in * convolved).astype(jnp.bfloat16)
    saved = (tiled, earlier, near_band, far_band, inside, across)
    return product, convolved, mixed, saved


def layer_backward(inputs, upstream, product, convolved, saved, skip_scale):
    tiled, earlier, near_band, far_band, inside, across = saved
    query_in = inputs[0].astype(jnp.float32)
    key_in = inputs[1].astype(jnp.float32)
    value_in = inputs[2].astype(jnp.float32)
    grad_up = upstream.astype(jnp.float32)
    gate_low = (grad_up * query_in).astype(jnp.bfloat16)
    gate_f = lax.optimization_barrier(gate_low).astype(jnp.float32)
    grad_tiles = gate_f.reshape(tiled.shape)
    following = jnp.concatenate([grad_tiles[1:], jnp.zeros_like(grad_tiles[:1])], 0)
    spread = jnp.einsum("gji,njgc->nigc", near_band, grad_tiles, precision=HIGH)
    spread = spread + jnp.einsum("gji,njgc->nigc", far_band, following, precision=HIGH)
    spread = spread.reshape(product.shape) + skip_scale * gate_f
    grad_inputs = jnp.stack([(grad_up * convolved).astype(jnp.bfloat16),
                             (spread * value_in).astype(jnp.bfloat16),
                             (spread * key_in).astype(jnp.bfloat16)])
    cross_near = jnp.einsum("nigc,njgc->gij", grad_tiles, tiled, precision=HIGH)
    cross_far = jnp.einsum("nigc,njgc->gij", grad_tiles, earlier, precision=HIGH)
    grad_kernel = jnp.einsum("gij,ijs->gs", cross_near, inside, precision=HIGH)
    grad_kernel = grad_kernel + jnp.einsum("gij,ijs->gs", cross_far, across, precision=HIGH)
    grad_skip = jnp.sum(gate_f * product, axis=0)
    return grad_inputs, grad_kernel, grad_skip


def reference(inputs_se, cotangent_se, kernel_se, skip_se, inputs_mr, kernel_mr, skip_mr, out_weight, cotangent_out):
    product_se, conv_se, mixed_se, saved_se = layer_forward(inputs_se, kernel_se, skip_se)
    grad_inputs_se, grad_kernel_se, grad_skip_se = layer_backward(inputs_se, cotangent_se, product_se, conv_se, saved_se, skip_se)
    product_mr, conv_mr, mixed_mr, saved_mr = layer_forward(inputs_mr, kernel_mr, skip_mr)
    weight_f = out_weight.astype(jnp.float32)
    mixed_f = mixed_mr.astype(jnp.float32)
    cotangent_f = cotangent_out.astype(jnp.float32)
    projected = jnp.dot(mixed_f, weight_f, precision=HIGH).astype(jnp.bfloat16)
    upstream_mr = jnp.dot(cotangent_f, weight_f.T, precision=HIGH).astype(jnp.bfloat16)
    grad_inputs_mr, grad_kernel_mr, grad_skip_mr = layer_backward(inputs_mr, upstream_mr, product_mr, conv_mr, saved_mr, skip_mr)
    mixed_blocks = mixed_f.reshape(N_CTX, TOK_DEV, D)
    cotangent_blocks = cotangent_f.reshape(N_CTX, TOK_DEV, OUT_W)

    def add_block(total, pair):
        left_part, right_part = pair
        term = lax.dot_general(left_part, right_part, (((0,), (0,)), ((), ())), precision=HIGH)
        term_low = term.astype(jnp.bfloat16)
        return total + term_low.astype(jnp.float32), None

    grad_out_weight, _ = lax.scan(add_block, jnp.zeros((D, OUT_W), jnp.float32), (mixed_blocks, cotangent_blocks))
    return (mixed_se, projected, grad_inputs_se, grad_inputs_mr, grad_kernel_se, grad_kernel_mr,
            grad_skip_se, grad_skip_mr, grad_out_weight)
```

```python
import jax
import jax.numpy as jnp
from jax import lax
from jax.experimental import pallas as pl
from jax.experimental.pallas import tpu as pltpu
from jax.sharding import PartitionSpec as P

GROUP = 16
LANES = 256
F32 = jnp.float32
BF16 = jnp.bfloat16


def lane_group(rows):
    return lax.broadcasted_iota(jnp.int32, (rows, LANES), 1) // GROUP


def banded(base_ref, data, taps):
    owner = lane_group(taps)
    total = jnp.zeros((taps, LANES), F32)
    for g in range(LANES // GROUP):
        row = jnp.broadcast_to(base_ref[g : g + 1, :], (taps, 2 * taps))
        band = pltpu.roll(row, 0, 1, stride=1, stride_axis=0).astype(BF16)
        part = jnp.dot(band, data, preferred_element_type=F32)
        total = jnp.where(owner == g, part, total)
    return total


def mr_forward_kernel(inputs_ref, before_ref, base_ref, skip_ref, conv_ref, mixed_ref):
    taps = before_ref.shape[0]
    product = (inputs_ref[1].astype(F32) * inputs_ref[2].astype(F32)).astype(BF16)
    data = jnp.concatenate([before_ref[...], product], 0)
    conv = banded(base_ref, data, taps) + skip_ref[...] * product.astype(F32)
    conv_ref[...] = conv
    mixed_ref[...] = (inputs_ref[0].astype(F32) * conv).astype(BF16)


def mr_forward(inputs, before, base, skip):
    _, rows, channels = inputs.shape
    return pl.pallas_call(
        mr_forward_kernel,
        grid=(channels // LANES,),
        in_specs=[
            pl.BlockSpec((3, rows, LANES), lambda i: (0, 0, i)),
            pl.BlockSpec((rows, LANES), lambda i: (0, i)),
            pl.BlockSpec((LANES // GROUP, 2 * rows), lambda i: (i, 0)),
            pl.BlockSpec((1, LANES), lambda i: (0, i)),
        ],
        out_specs=[
            pl.BlockSpec((rows, LANES), lambda i: (0, i)),
            pl.BlockSpec((rows, LANES), lambda i: (0, i)),
        ],
        out_shape=[
            jax.ShapeDtypeStruct((rows, channels), F32),
            jax.ShapeDtypeStruct((rows, channels), BF16),
        ],
        compiler_params=pltpu.CompilerParams(vmem_limit_bytes=32 * 2**20),
        cost_estimate=pl.CostEstimate(
            flops=4 * rows * rows * channels * GROUP, bytes_accessed=11 * rows * channels,
            transcendentals=0,
        ),
        name="mr_forward",
    )(inputs, before, base, skip)


def mr_backward_kernel(
    inputs_ref, before_ref, upstream_ref, after_ref, conv_ref, base_ref, skip_ref,
    grads_ref, cross_ref, skip_grad_ref,
):
    taps = before_ref.shape[0]
    product = (inputs_ref[1].astype(F32) * inputs_ref[2].astype(F32)).astype(BF16)
    data = jnp.concatenate([before_ref[...], product], 0)
    upstream = upstream_ref[...].astype(F32)
    gate = (upstream * inputs_ref[0].astype(F32)).astype(BF16)
    gate_f = gate.astype(F32)
    spread = banded(base_ref, jnp.concatenate([gate, after_ref[...]], 0), taps)
    spread = spread + skip_ref[...] * gate_f
    grads_ref[0] = (upstream * conv_ref[...]).astype(BF16)
    grads_ref[1] = (spread * inputs_ref[2].astype(F32)).astype(BF16)
    grads_ref[2] = (spread * inputs_ref[1].astype(F32)).astype(BF16)
    skip_grad_ref[...] = jnp.sum(gate_f * product.astype(F32), axis=0, keepdims=True)
    owner = lane_group(taps)
    for g in range(LANES // GROUP):
        kept = jnp.where(owner == g, gate_f, 0.0).astype(BF16)
        cross = lax.dot_general(
            kept, data, (((1,), (1,)), ((), ())), preferred_element_type=F32
        )
        total = cross[0:8]
        for a in range(1, taps // 8):
            total = total + pltpu.roll(cross[8 * a : 8 * a + 8], 2 * taps - 8 * a, 1)
        cross_ref[g] = total


def mr_backward(inputs, before, upstream, after, conv, base, skip):
    _, rows, channels = inputs.shape
    flat = pl.BlockSpec((rows, LANES), lambda i: (0, i))
    cube = pl.BlockSpec((3, rows, LANES), lambda i: (0, 0, i))
    line = pl.BlockSpec((1, LANES), lambda i: (0, i))
    return pl.pallas_call(
        mr_backward_kernel,
        grid=(channels // LANES,),
        in_specs=[
            cube, flat, flat, flat, flat,
            pl.BlockSpec((LANES // GROUP, 2 * rows), lambda i: (i, 0)),
            line,
        ],
        out_specs=[
            cube,
            pl.BlockSpec((LANES // GROUP, 8, 2 * rows), lambda i: (i, 0, 0)),
            line,
        ],
        out_shape=[
            jax.ShapeDtypeStruct((3, rows, channels), BF16),
            jax.ShapeDtypeStruct((channels // GROUP, 8, 2 * rows), F32),
            jax.ShapeDtypeStruct((1, channels), F32),
        ],
        compiler_params=pltpu.CompilerParams(vmem_limit_bytes=32 * 2**20),
        cost_estimate=pl.CostEstimate(
            flops=8 * rows * rows * channels * GROUP, bytes_accessed=24 * rows * channels,
            transcendentals=0,
        ),
        name="mr_backward",
    )(inputs, before, upstream, after, conv, base, skip)


def se_kernel(
    taps, inputs_ref, cotangent_ref, before_ref, after_ref, filter_ref, skip_ref,
    mixed_ref, grads_ref, sums_ref,
):
    rows = cotangent_ref.shape[0]
    query = inputs_ref[0].astype(F32)
    cotangent = cotangent_ref[...].astype(F32)
    key = inputs_ref[1].astype(F32)
    value = inputs_ref[2].astype(F32)
    product = (key * value).astype(BF16).astype(F32)
    gate = (cotangent * query).astype(BF16).astype(F32)
    earlier = jnp.concatenate([before_ref[...], product], 0)
    later = jnp.concatenate([gate, after_ref[...]], 0)
    pad = before_ref.shape[0]
    conv = skip_ref[...] * product
    spread = skip_ref[...] * gate
    sums = []
    for s in range(taps):
        weight = filter_ref[s : s + 1, :]
        moved = earlier[pad - s : pad - s + rows]
        conv = conv + weight * moved
        spread = spread + weight * later[s : s + rows]
        sums.append(jnp.sum(gate * moved, axis=0, keepdims=True))
    sums.append(jnp.zeros((sums_ref.shape[0] - taps, sums[0].shape[1]), F32))
    sums_ref[...] = jnp.concatenate(sums, 0)
    mixed_ref[...] = (query * conv).astype(BF16)
    grads_ref[0] = (cotangent * conv).astype(BF16)
    grads_ref[1] = (spread * value).astype(BF16)
    grads_ref[2] = (spread * key).astype(BF16)


def se_operator(inputs, cotangent, before, after, filters, skip, taps):
    _, rows, channels = inputs.shape
    halo = before.shape[0]
    flat = pl.BlockSpec((rows, LANES), lambda i: (0, i))
    cube = pl.BlockSpec((3, rows, LANES), lambda i: (0, 0, i))
    line = pl.BlockSpec((1, LANES), lambda i: (0, i))
    edge = pl.BlockSpec((halo, LANES), lambda i: (0, i))

    def kernel(*refs):
        se_kernel(taps, *refs)

    return pl.pallas_call(
        kernel,
        grid=(channels // LANES,),
        in_specs=[cube, flat, edge, edge, edge, line],
        out_specs=[flat, cube, edge],
        out_shape=[
            jax.ShapeDtypeStruct((rows, channels), BF16),
            jax.ShapeDtypeStruct((3, rows, channels), BF16),
            jax.ShapeDtypeStruct((halo, channels), F32),
        ],
        compiler_params=pltpu.CompilerParams(vmem_limit_bytes=32 * 2**20),
        cost_estimate=pl.CostEstimate(
            flops=50 * rows * channels, bytes_accessed=16 * rows * channels, transcendentals=0
        ),
        name="se_operator",
    )(inputs, cotangent, before, after, filters, skip)


def gated(left, right):
    return (left.astype(F32) * right.astype(F32)).astype(BF16)


def on_device(
    inputs_se, cotangent_se, kernel_se, skip_se, inputs_mr, kernel_mr, skip_mr, out_weight,
    cotangent_out,
):
    count = lax.axis_size("ctx")
    up = [(i, i + 1) for i in range(count - 1)]
    down = [(i + 1, i) for i in range(count - 1)]
    rows = inputs_mr.shape[1]
    channels = inputs_mr.shape[2]
    groups = channels // GROUP
    taps_se = kernel_se.shape[1]
    halo = 8

    wide = lax.all_gather(cotangent_out, "grp", axis=1, tiled=True)
    columns = lax.all_to_all(wide, "ctx", split_axis=1, concat_axis=0, tiled=True)
    term = lax.dot_general(
        columns, out_weight, (((1,), (1,)), ((), ())), preferred_element_type=F32
    ).astype(BF16)
    upstream = lax.psum_scatter(term, "ctx", scatter_dimension=0, tiled=True)

    before_mr = lax.ppermute(gated(inputs_mr[1], inputs_mr[2]), "ctx", up)
    before_se = lax.ppermute(
        gated(inputs_se[1, rows - halo :], inputs_se[2, rows - halo :]), "ctx", up
    )
    after_se = lax.ppermute(gated(cotangent_se[:halo], inputs_se[0, :halo]), "ctx", down)

    taps_f = kernel_mr.astype(F32)
    blank = jnp.zeros((groups, 1), F32)
    base_forward = jnp.concatenate(
        [blank, taps_f[:, ::-1], jnp.zeros((groups, rows - 1), F32)], 1
    )
    base_backward = jnp.concatenate([taps_f, jnp.zeros((groups, rows), F32)], 1)
    conv_mr, mixed_mr = mr_forward(inputs_mr, before_mr, base_forward, skip_mr[None])
    gathered = lax.all_gather(mixed_mr, "ctx", axis=0, tiled=True)

    filters = jnp.repeat(kernel_se.astype(F32).T, GROUP, axis=1)
    filters = jnp.concatenate([filters, jnp.zeros((halo - taps_se, channels), F32)], 0)
    mixed_se, grads_se, sums_se = se_operator(
        inputs_se, cotangent_se, before_se.astype(F32), after_se.astype(F32), filters,
        skip_se[None], taps_se,
    )

    after_mr = lax.ppermute(gated(upstream, inputs_mr[0]), "ctx", down)
    grads_mr, cross, skip_part_mr = mr_backward(
        inputs_mr, before_mr, upstream, after_mr, conv_mr, base_backward, skip_mr[None]
    )
    diagonals = cross[:, 0, 1 : rows + 1]
    for b in range(1, 8):
        diagonals = diagonals + cross[:, b, b + 1 : b + rows + 1]
    kernel_part_mr = diagonals[:, ::-1]
    kernel_part_se = sums_se.reshape(halo, groups, GROUP).sum(2).T
    packed = jnp.concatenate(
        [
            kernel_part_mr,
            kernel_part_se,
            sums_se[0].reshape(groups, GROUP),
            skip_part_mr.reshape(groups, GROUP),
        ],
        1,
    )
    packed = lax.psum(packed, "ctx")
    at = rows + halo
    grad_kernel_mr = packed[:, :rows]
    grad_kernel_se = packed[:, rows : rows + taps_se]
    grad_skip_se = packed[:, at : at + GROUP].reshape(channels)
    grad_skip_mr = packed[:, at + GROUP : at + 2 * GROUP].reshape(channels)

    partial_value = jnp.dot(gathered, out_weight, preferred_element_type=F32).astype(BF16)
    grad_out_weight = lax.dot_general(
        gathered, columns, (((0,), (0,)), ((), ())), preferred_element_type=F32
    )
    spread_value = lax.all_to_all(partial_value, "ctx", split_axis=0, concat_axis=1, tiled=True)
    projected = lax.psum_scatter(spread_value, "grp", scatter_dimension=1, tiled=True)
    return (
        mixed_se, projected, grads_se, grads_mr, grad_kernel_se, grad_kernel_mr, grad_skip_se,
        grad_skip_mr, grad_out_weight,
    )


def solution(mesh):
    placed = (
        P(None, "ctx", "grp"),
        P("ctx", "grp"),
        P("grp", None),
        P("grp"),
        P(None, "ctx", "grp"),
        P("grp", None),
        P("grp"),
        P("grp", "ctx"),
        P("ctx", "grp"),
    )
    return jax.shard_map(
        on_device,
        mesh=mesh,
        in_specs=placed,
        out_specs=(
            P("ctx", "grp"),
            P("ctx", "grp"),
            P(None, "ctx", "grp"),
            P(None, "ctx", "grp"),
            P("grp", None),
            P("grp", None),
            P("grp"),
            P("grp"),
            P("grp", "ctx"),
        ),
        check_vma=False,
    )
```

```python
import jax
import jax.numpy as jnp
from jax import lax
from jax.experimental import pallas as pl
from jax.experimental.pallas import tpu as pltpu
from jax.sharding import PartitionSpec as P

GROUP = 16
LANES = 256
F32 = jnp.float32
BF16 = jnp.bfloat16


def lane_group(rows):
    return lax.broadcasted_iota(jnp.int32, (rows, LANES), 1) // GROUP


def banded(base_ref, data, taps):
    owner = lane_group(taps)
    total = jnp.zeros((taps, LANES), F32)
    for g in range(LANES // GROUP):
        row = jnp.broadcast_to(base_ref[g : g + 1, :], (taps, 2 * taps))
        band = pltpu.roll(row, 0, 1, stride=1, stride_axis=0).astype(BF16)
        part = jnp.dot(band, data, preferred_element_type=F32)
        total = jnp.where(owner == g, part, total)
    return total


def mr_forward_kernel(inputs_ref, before_ref, base_ref, skip_ref, conv_ref, mixed_ref):
    taps = before_ref.shape[0]
    product = (inputs_ref[1].astype(F32) * inputs_ref[2].astype(F32)).astype(BF16)
    data = jnp.concatenate([before_ref[...], product], 0)
    conv = banded(base_ref, data, taps) + skip_ref[...] * product.astype(F32)
    conv_ref[...] = conv
    mixed_ref[...] = (inputs_ref[0].astype(F32) * conv).astype(BF16)


def mr_forward(inputs, before, base, skip):
    _, rows, channels = inputs.shape
    return pl.pallas_call(
        mr_forward_kernel,
        grid=(channels // LANES,),
        in_specs=[
            pl.BlockSpec((3, rows, LANES), lambda i: (0, 0, i)),
            pl.BlockSpec((rows, LANES), lambda i: (0, i)),
            pl.BlockSpec((LANES // GROUP, 2 * rows), lambda i: (i, 0)),
            pl.BlockSpec((1, LANES), lambda i: (0, i)),
        ],
        out_specs=[
            pl.BlockSpec((rows, LANES), lambda i: (0, i)),
            pl.BlockSpec((rows, LANES), lambda i: (0, i)),
        ],
        out_shape=[
            jax.ShapeDtypeStruct((rows, channels), F32),
            jax.ShapeDtypeStruct((rows, channels), BF16),
        ],
        compiler_params=pltpu.CompilerParams(vmem_limit_bytes=32 * 2**20),
        cost_estimate=pl.CostEstimate(
            flops=4 * rows * rows * channels * GROUP, bytes_accessed=11 * rows * channels,
            transcendentals=0,
        ),
        name="mr_forward",
    )(inputs, before, base, skip)


def mr_backward_kernel(
    inputs_ref, before_ref, upstream_ref, after_ref, conv_ref, base_ref, skip_ref,
    grads_ref, cross_ref, skip_grad_ref,
):
    taps = before_ref.shape[0]
    product = (inputs_ref[1].astype(F32) * inputs_ref[2].astype(F32)).astype(BF16)
    data = jnp.concatenate([before_ref[...], product], 0)
    upstream = upstream_ref[...].astype(F32)
    gate = (upstream * inputs_ref[0].astype(F32)).astype(BF16)
    gate_f = gate.astype(F32)
    spread = banded(base_ref, jnp.concatenate([gate, after_ref[...]], 0), taps)
    spread = spread + skip_ref[...] * gate_f
    grads_ref[0] = (upstream * conv_ref[...]).astype(BF16)
    grads_ref[1] = (spread * inputs_ref[2].astype(F32)).astype(BF16)
    grads_ref[2] = (spread * inputs_ref[1].astype(F32)).astype(BF16)
    skip_grad_ref[...] = jnp.sum(gate_f * product.astype(F32), axis=0, keepdims=True)
    owner = lane_group(taps)
    for g in range(LANES // GROUP):
        kept = jnp.where(owner == g, gate_f, 0.0).astype(BF16)
        cross = lax.dot_general(
            kept, data, (((1,), (1,)), ((), ())), preferred_element_type=F32
        )
        total = cross[0:8]
        for a in range(1, taps // 8):
            total = total + pltpu.roll(cross[8 * a : 8 * a + 8], 2 * taps - 8 * a, 1)
        cross_ref[g] = total


def mr_backward(inputs, before, upstream, after, conv, base, skip):
    _, rows, channels = inputs.shape
    flat = pl.BlockSpec((rows, LANES), lambda i: (0, i))
    cube = pl.BlockSpec((3, rows, LANES), lambda i: (0, 0, i))
    line = pl.BlockSpec((1, LANES), lambda i: (0, i))
    return pl.pallas_call(
        mr_backward_kernel,
        grid=(channels // LANES,),
        in_specs=[
            cube, flat, flat, flat, flat,
            pl.BlockSpec((LANES // GROUP, 2 * rows), lambda i: (i, 0)),
            line,
        ],
        out_specs=[
            cube,
            pl.BlockSpec((LANES // GROUP, 8, 2 * rows), lambda i: (i, 0, 0)),
            line,
        ],
        out_shape=[
            jax.ShapeDtypeStruct((3, rows, channels), BF16),
            jax.ShapeDtypeStruct((channels // GROUP, 8, 2 * rows), F32),
            jax.ShapeDtypeStruct((1, channels), F32),
        ],
        compiler_params=pltpu.CompilerParams(vmem_limit_bytes=32 * 2**20),
        cost_estimate=pl.CostEstimate(
            flops=8 * rows * rows * channels * GROUP, bytes_accessed=24 * rows * channels,
            transcendentals=0,
        ),
        name="mr_backward",
    )(inputs, before, upstream, after, conv, base, skip)


def se_kernel(
    taps, inputs_ref, cotangent_ref, before_ref, after_ref, filter_ref, skip_ref,
    mixed_ref, grads_ref, sums_ref,
):
    rows = cotangent_ref.shape[0]
    query = inputs_ref[0].astype(F32)
    cotangent = cotangent_ref[...].astype(F32)
    key = inputs_ref[1].astype(F32)
    value = inputs_ref[2].astype(F32)
    product = (key * value).astype(BF16).astype(F32)
    gate = (cotangent * query).astype(BF16).astype(F32)
    earlier = jnp.concatenate([before_ref[...], product], 0)
    later = jnp.concatenate([gate, after_ref[...]], 0)
    pad = before_ref.shape[0]
    conv = skip_ref[...] * product
    spread = skip_ref[...] * gate
    sums = []
    for s in range(taps):
        weight = filter_ref[s : s + 1, :]
        moved = earlier[pad - s : pad - s + rows]
        conv = conv + weight * moved
        spread = spread + weight * later[s : s + rows]
        sums.append(jnp.sum(gate * moved, axis=0, keepdims=True))
    sums.append(jnp.zeros((sums_ref.shape[0] - taps, sums[0].shape[1]), F32))
    sums_ref[...] = jnp.concatenate(sums, 0)
    mixed_ref[...] = (query * conv).astype(BF16)
    grads_ref[0] = (cotangent * conv).astype(BF16)
    grads_ref[1] = (spread * value).astype(BF16)
    grads_ref[2] = (spread * key).astype(BF16)


def se_operator(inputs, cotangent, before, after, filters, skip, taps):
    _, rows, channels = inputs.shape
    halo = before.shape[0]
    flat = pl.BlockSpec((rows, LANES), lambda i: (0, i))
    cube = pl.BlockSpec((3, rows, LANES), lambda i: (0, 0, i))
    line = pl.BlockSpec((1, LANES), lambda i: (0, i))
    edge = pl.BlockSpec((halo, LANES), lambda i: (0, i))

    def kernel(*refs):
        se_kernel(taps, *refs)

    return pl.pallas_call(
        kernel,
        grid=(channels // LANES,),
        in_specs=[cube, flat, edge, edge, edge, line],
        out_specs=[flat, cube, edge],
        out_shape=[
            jax.ShapeDtypeStruct((rows, channels), BF16),
            jax.ShapeDtypeStruct((3, rows, channels), BF16),
            jax.ShapeDtypeStruct((halo, channels), F32),
        ],
        compiler_params=pltpu.CompilerParams(vmem_limit_bytes=32 * 2**20),
        cost_estimate=pl.CostEstimate(
            flops=50 * rows * channels, bytes_accessed=16 * rows * channels, transcendentals=0
        ),
        name="se_operator",
    )(inputs, cotangent, before, after, filters, skip)


MESH = pl.DeviceIdType.MESH


def greet_all(n, m, me, mine):
    barrier = pltpu.get_barrier_semaphore()

    def one(k, carry):
        there = lax.rem(me * m + mine + k, n * m)
        pl.semaphore_signal(
            barrier, inc=1, device_id=(there // m, lax.rem(there, m)), device_id_type=MESH
        )
        return carry

    lax.fori_loop(1, n * m, one, 0)
    pl.semaphore_wait(barrier, n * m - 1)


def ring_kernel(
    n, m, tile, cot_ref, weight_ref, out_ref, columns_ref, cols, sib, weight_sib, sums, outgoing,
    incoming, cot_send, cot_recv, local_sem, pair_send, pair_recv, ring_send, ring_recv,
):
    me, mine = lax.axis_index("ctx"), lax.axis_index("grp")
    rows = cot_ref.shape[0]
    channels, width = weight_ref.shape
    per = cot_ref.shape[1] // width
    half, hops = rows // 2, n // 2
    core, chip = lax.rem(me, 2), me // 2
    sibling = me + 1 - 2 * core
    depth = hops // 2

    def chip_at(place):
        turn = place // depth
        z = (1 - turn) * place + turn * (2 * depth - 1 - place)
        return 2 * z + turn

    x, z = lax.rem(chip, 2), chip // 2
    place = (1 - x) * z + x * (2 * depth - 1 - z)
    right = 2 * chip_at(lax.rem(place + 1, hops)) + core
    left = 2 * chip_at(lax.rem(place + hops - 1, hops)) + core
    greet_all(n, m, me, mine)

    def pair_copy(source, target, k):
        return pltpu.make_async_remote_copy(
            src_ref=source, dst_ref=target, send_sem=pair_send.at[k], recv_sem=pair_recv.at[k],
            device_id=(sibling, mine), device_id_type=MESH,
        )

    weight_copy = pair_copy(weight_ref, weight_sib, 0)
    weight_copy.start()

    def cot_copy(b, g, source):
        return pltpu.make_async_remote_copy(
            src_ref=cot_ref.at[:, b * width : (b + 1) * width],
            dst_ref=cols.at[lax.rem(source, 2), source // 2],
            send_sem=cot_send.at[b, g], recv_sem=cot_recv.at[source],
            device_id=(mine * per + b, g), device_id_type=MESH,
        )

    for b in range(per):
        for g in range(m):
            own = jnp.logical_and(mine * per + b == me, mine == g)

            @pl.when(jnp.logical_not(own))
            def _(b=b, g=g):
                cot_copy(b, g, me).start()

            @pl.when(own)
            def _(b=b):
                copy = pltpu.make_async_copy(
                    cot_ref.at[:, b * width : (b + 1) * width], cols.at[core, chip], local_sem
                )
                copy.start()
                copy.wait()

    def arrive(source, carry):
        own = jnp.logical_and(source == me, me // per == mine)

        @pl.when(jnp.logical_not(own))
        def _():
            cot_copy(0, 0, source).wait_recv()

        return carry

    lax.fori_loop(0, n, arrive, 0)
    cols_copy = pair_copy(cols.at[1 - core], sib, 1)
    cols_copy.start()
    columns_ref[...] = cols[...]
    weight_copy.wait_recv()
    cols_copy.wait_recv()

    def terms(owners):
        def one(t, carry):
            at = pl.ds(pl.multiple_of(t * tile, tile), tile)
            for d in range(2):
                part = pl.ds(d * half, half)
                dims = (((1,), (1,)), ((), ()))
                near = lax.dot_general(
                    cols[core, owners[d], part, :], weight_ref[at, :], dims,
                    preferred_element_type=F32,
                )
                far = lax.dot_general(
                    sib[owners[d], part, :], weight_sib[at, :], dims, preferred_element_type=F32
                )
                sums[d, :, at] = near + far
            return carry

        lax.fori_loop(0, channels // tile, one, 0)

    def hop(d, s):
        return pltpu.make_async_remote_copy(
            src_ref=outgoing.at[d, s], dst_ref=incoming.at[d, s],
            send_sem=ring_send.at[d, s], recv_sem=ring_recv.at[d, s],
            device_id=((right, left)[d], mine), device_id_type=MESH,
        )

    def owners_at(s):
        return (
            chip_at(lax.rem(place + 2 * hops - 1 - s, hops)),
            chip_at(lax.rem(place + 1 + s, hops)),
        )

    terms(owners_at(0))
    for d in range(2):
        outgoing[d, 0] = sums[d].astype(BF16)
        hop(d, 0).start()

    def step(s, carry):
        terms(owners_at(s))
        for d in range(2):
            hop(d, s - 1).wait_recv()
            outgoing[d, s] = (sums[d] + incoming[d, s - 1].astype(F32)).astype(BF16)
            hop(d, s).start()
        return carry

    lax.fori_loop(1, hops - 1, step, 0)
    terms((chip, chip))
    for d in range(2):
        hop(d, hops - 2).wait_recv()
        out_ref[d * half : (d + 1) * half] = (
            sums[d] + incoming[d, hops - 2].astype(F32)
        ).astype(BF16)

    def sent(s, carry):
        for d in range(2):
            hop(d, s).wait_send()
        return carry

    lax.fori_loop(0, hops - 1, sent, 0)
    weight_copy.wait_send()
    cols_copy.wait_send()
    for b in range(per):
        for g in range(m):
            own = jnp.logical_and(mine * per + b == me, mine == g)

            @pl.when(jnp.logical_not(own))
            def _(b=b, g=g):
                cot_copy(b, g, me).wait_send()


def ring_upstream(cotangent, weight):
    n, m = lax.axis_size("ctx"), lax.axis_size("grp")
    rows = cotangent.shape[0]
    channels, width = weight.shape
    hops, half = n // 2, rows // 2
    tile = min(512, channels)
    dma = pltpu.SemaphoreType.DMA

    def kernel(*refs):
        ring_kernel(n, m, tile, *refs)

    vmem = pl.BlockSpec(memory_space=pltpu.VMEM)
    upstream, columns = pl.pallas_call(
        kernel,
        in_specs=[vmem, vmem],
        out_specs=[vmem, vmem],
        out_shape=[
            jax.ShapeDtypeStruct((rows, channels), BF16),
            jax.ShapeDtypeStruct((2, hops, rows, width), BF16),
        ],
        scratch_shapes=[
            pltpu.VMEM((2, hops, rows, width), BF16),
            pltpu.VMEM((hops, rows, width), BF16),
            pltpu.VMEM((channels, width), BF16),
            pltpu.VMEM((2, half, channels), F32),
            pltpu.VMEM((2, hops - 1, half, channels), BF16),
            pltpu.VMEM((2, hops - 1, half, channels), BF16),
            dma((cotangent.shape[1] // width, m)), dma((n,)), dma,
            dma((2,)), dma((2,)), dma((2, hops - 1)), dma((2, hops - 1)),
        ],
        compiler_params=pltpu.CompilerParams(
            collective_id=0, has_side_effects=True, vmem_limit_bytes=44 * 2**20
        ),
        cost_estimate=pl.CostEstimate(
            flops=2 * n * rows * channels * width, bytes_accessed=300 * 2**20, transcendentals=0
        ),
        name="ring_upstream",
    )(cotangent, weight)
    return upstream, jnp.swapaxes(columns, 0, 1).reshape(n * rows, width)


def sum_kernel(n, m, part_ref, total_ref, landed, shared, first_send, first_recv, last_send, last_recv):
    me, mine = lax.axis_index("ctx"), lax.axis_index("grp")
    barrier = pltpu.get_barrier_semaphore()

    def greet(k, carry):
        pl.semaphore_signal(
            barrier, inc=1, device_id=(lax.rem(me + k, n), mine), device_id_type=MESH
        )
        return carry

    lax.fori_loop(1, n, greet, 0)
    pl.semaphore_wait(barrier, n - 1)

    def first(k, source):
        there = lax.rem(me + k, n)
        return pltpu.make_async_remote_copy(
            src_ref=part_ref.at[there], dst_ref=landed.at[source], send_sem=first_send.at[k],
            recv_sem=first_recv.at[source], device_id=(there, mine), device_id_type=MESH,
        )

    def last(k, source):
        there = lax.rem(me + k, n)
        return pltpu.make_async_remote_copy(
            src_ref=shared.at[me], dst_ref=shared.at[source], send_sem=last_send.at[k],
            recv_sem=last_recv.at[source], device_id=(there, mine), device_id_type=MESH,
        )

    def loop(body):
        def one(k, carry):
            body(k)
            return carry

        lax.fori_loop(1, n, one, 0)

    loop(lambda k: first(k, me).start())

    def add(k, total):
        source = lax.rem(me + k, n)
        first(k, source).wait_recv()
        return total + landed[source]

    shared[me] = lax.fori_loop(1, n, add, part_ref[me])
    loop(lambda k: last(k, me).start())
    loop(lambda k: last(k, lax.rem(me + k, n)).wait_recv())
    total_ref[...] = shared[...]
    loop(lambda k: first(k, me).wait_send())
    loop(lambda k: last(k, me).wait_send())


def sum_over_ctx(part):
    n, m = lax.axis_size("ctx"), lax.axis_size("grp")
    shape = (n, part.shape[0] // n, part.shape[1])
    dma = pltpu.SemaphoreType.DMA

    def kernel(*refs):
        sum_kernel(n, m, *refs)

    vmem = pl.BlockSpec(memory_space=pltpu.VMEM)
    total = pl.pallas_call(
        kernel,
        in_specs=[vmem],
        out_specs=vmem,
        out_shape=jax.ShapeDtypeStruct(shape, F32),
        scratch_shapes=[pltpu.VMEM(shape, F32), pltpu.VMEM(shape, F32)] + [dma((n,))] * 4,
        compiler_params=pltpu.CompilerParams(
            collective_id=1, has_side_effects=True, vmem_limit_bytes=16 * 2**20
        ),
        cost_estimate=pl.CostEstimate(
            flops=part.size, bytes_accessed=40 * 2**20, transcendentals=0
        ),
        name="sum_over_ctx",
    )(part.reshape(shape))
    return total.reshape(part.shape)


def gated(left, right):
    return (left.astype(F32) * right.astype(F32)).astype(BF16)


def on_device(
    inputs_se, cotangent_se, kernel_se, skip_se, inputs_mr, kernel_mr, skip_mr, out_weight,
    cotangent_out,
):
    count = lax.axis_size("ctx")
    up = [(i, i + 1) for i in range(count - 1)]
    down = [(i + 1, i) for i in range(count - 1)]
    rows = inputs_mr.shape[1]
    channels = inputs_mr.shape[2]
    groups = channels // GROUP
    taps_se = kernel_se.shape[1]
    halo = 8

    before_mr = lax.ppermute(gated(inputs_mr[1], inputs_mr[2]), "ctx", up)
    before_se = lax.ppermute(
        gated(inputs_se[1, rows - halo :], inputs_se[2, rows - halo :]), "ctx", up
    )
    after_se = lax.ppermute(gated(cotangent_se[:halo], inputs_se[0, :halo]), "ctx", down)

    taps_f = kernel_mr.astype(F32)
    blank = jnp.zeros((groups, 1), F32)
    base_forward = jnp.concatenate(
        [blank, taps_f[:, ::-1], jnp.zeros((groups, rows - 1), F32)], 1
    )
    base_backward = jnp.concatenate([taps_f, jnp.zeros((groups, rows), F32)], 1)
    conv_mr, mixed_mr = mr_forward(inputs_mr, before_mr, base_forward, skip_mr[None])
    upstream, columns = ring_upstream(cotangent_out, out_weight)
    mixed_mr, upstream = lax.optimization_barrier((mixed_mr, upstream))
    gathered = lax.all_gather(mixed_mr, "ctx", axis=0, tiled=True)

    filters = jnp.repeat(kernel_se.astype(F32).T, GROUP, axis=1)
    filters = jnp.concatenate([filters, jnp.zeros((halo - taps_se, channels), F32)], 0)
    mixed_se, grads_se, sums_se = se_operator(
        inputs_se, cotangent_se, before_se.astype(F32), after_se.astype(F32), filters,
        skip_se[None], taps_se,
    )

    after_mr = lax.ppermute(gated(upstream, inputs_mr[0]), "ctx", down)
    grads_mr, cross, skip_part_mr = mr_backward(
        inputs_mr, before_mr, upstream, after_mr, conv_mr, base_backward, skip_mr[None]
    )
    diagonals = cross[:, 0, 1 : rows + 1]
    for b in range(1, 8):
        diagonals = diagonals + cross[:, b, b + 1 : b + rows + 1]
    kernel_part_mr = diagonals[:, ::-1]
    kernel_part_se = sums_se.reshape(halo, groups, GROUP).sum(2).T
    packed = jnp.concatenate(
        [
            kernel_part_mr,
            kernel_part_se,
            sums_se[0].reshape(groups, GROUP),
            skip_part_mr.reshape(groups, GROUP),
            jnp.zeros((groups, -(rows + halo + 2 * GROUP) % 128), F32),
        ],
        1,
    )
    packed = sum_over_ctx(packed)
    packed, gathered = lax.optimization_barrier((packed, gathered))
    at = rows + halo
    grad_kernel_mr = packed[:, :rows]
    grad_kernel_se = packed[:, rows : rows + taps_se]
    grad_skip_se = packed[:, at : at + GROUP].reshape(channels)
    grad_skip_mr = packed[:, at + GROUP : at + 2 * GROUP].reshape(channels)

    partial_value = jnp.dot(gathered, out_weight, preferred_element_type=F32).astype(BF16)
    grad_out_weight = lax.dot_general(
        gathered, columns, (((0,), (0,)), ((), ())), preferred_element_type=F32
    )
    spread_value = lax.all_to_all(partial_value, "ctx", split_axis=0, concat_axis=1, tiled=True)
    projected = lax.psum_scatter(spread_value, "grp", scatter_dimension=1, tiled=True)
    return (
        mixed_se, projected, grads_se, grads_mr, grad_kernel_se, grad_kernel_mr, grad_skip_se,
        grad_skip_mr, grad_out_weight,
    )


def solution(mesh):
    placed = (
        P(None, "ctx", "grp"),
        P("ctx", "grp"),
        P("grp", None),
        P("grp"),
        P(None, "ctx", "grp"),
        P("grp", None),
        P("grp"),
        P("grp", "ctx"),
        P("ctx", "grp"),
    )
    return jax.shard_map(
        on_device,
        mesh=mesh,
        in_specs=placed,
        out_specs=(
            P("ctx", "grp"),
            P("ctx", "grp"),
            P(None, "ctx", "grp"),
            P(None, "ctx", "grp"),
            P("grp", None),
            P("grp", None),
            P("grp"),
            P("grp"),
            P("grp", "ctx"),
        ),
        check_vma=False,
    )
```

```python
import jax
import jax.numpy as jnp
from jax import lax
from jax.experimental import pallas as pl
from jax.experimental.pallas import tpu as pltpu
from jax.sharding import PartitionSpec as P

GROUP = 16
LANES = 256
F32 = jnp.float32
BF16 = jnp.bfloat16


def lane_group(rows):
    return lax.broadcasted_iota(jnp.int32, (rows, LANES), 1) // GROUP


def banded(base_ref, data, taps):
    owner = lane_group(taps)
    total = jnp.zeros((taps, LANES), F32)
    for g in range(LANES // GROUP):
        row = jnp.broadcast_to(base_ref[g : g + 1, :], (taps, 2 * taps))
        band = pltpu.roll(row, 0, 1, stride=1, stride_axis=0).astype(BF16)
        part = jnp.dot(band, data, preferred_element_type=F32)
        total = jnp.where(owner == g, part, total)
    return total


def mr_forward_kernel(inputs_ref, before_ref, base_ref, skip_ref, conv_ref, mixed_ref):
    taps = before_ref.shape[0]
    product = (inputs_ref[1].astype(F32) * inputs_ref[2].astype(F32)).astype(BF16)
    data = jnp.concatenate([before_ref[...], product], 0)
    conv = banded(base_ref, data, taps) + skip_ref[...] * product.astype(F32)
    conv_ref[...] = conv
    mixed_ref[...] = (inputs_ref[0].astype(F32) * conv).astype(BF16)


def mr_forward(inputs, before, base, skip):
    _, rows, channels = inputs.shape
    return pl.pallas_call(
        mr_forward_kernel,
        grid=(channels // LANES,),
        in_specs=[
            pl.BlockSpec((3, rows, LANES), lambda i: (0, 0, i)),
            pl.BlockSpec((rows, LANES), lambda i: (0, i)),
            pl.BlockSpec((LANES // GROUP, 2 * rows), lambda i: (i, 0)),
            pl.BlockSpec((1, LANES), lambda i: (0, i)),
        ],
        out_specs=[
            pl.BlockSpec((rows, LANES), lambda i: (0, i)),
            pl.BlockSpec((rows, LANES), lambda i: (0, i)),
        ],
        out_shape=[
            jax.ShapeDtypeStruct((rows, channels), F32),
            jax.ShapeDtypeStruct((rows, channels), BF16),
        ],
        compiler_params=pltpu.CompilerParams(vmem_limit_bytes=32 * 2**20),
        cost_estimate=pl.CostEstimate(
            flops=4 * rows * rows * channels * GROUP, bytes_accessed=11 * rows * channels,
            transcendentals=0,
        ),
        name="mr_forward",
    )(inputs, before, base, skip)


def mr_backward_kernel(
    inputs_ref, before_ref, upstream_ref, after_ref, conv_ref, base_ref, skip_ref,
    grads_ref, cross_ref, skip_grad_ref,
):
    taps = before_ref.shape[0]
    product = (inputs_ref[1].astype(F32) * inputs_ref[2].astype(F32)).astype(BF16)
    data = jnp.concatenate([before_ref[...], product], 0)
    upstream = upstream_ref[...].astype(F32)
    gate = (upstream * inputs_ref[0].astype(F32)).astype(BF16)
    gate_f = gate.astype(F32)
    spread = banded(base_ref, jnp.concatenate([gate, after_ref[...]], 0), taps)
    spread = spread + skip_ref[...] * gate_f
    grads_ref[0] = (upstream * conv_ref[...]).astype(BF16)
    grads_ref[1] = (spread * inputs_ref[2].astype(F32)).astype(BF16)
    grads_ref[2] = (spread * inputs_ref[1].astype(F32)).astype(BF16)
    skip_grad_ref[...] = jnp.sum(gate_f * product.astype(F32), axis=0, keepdims=True)
    owner = lane_group(taps)
    for g in range(LANES // GROUP):
        kept = jnp.where(owner == g, gate_f, 0.0).astype(BF16)
        cross = lax.dot_general(
            kept, data, (((1,), (1,)), ((), ())), preferred_element_type=F32
        )
        total = cross[0:8]
        for a in range(1, taps // 8):
            total = total + pltpu.roll(cross[8 * a : 8 * a + 8], 2 * taps - 8 * a, 1)
        cross_ref[g] = total


def mr_backward(inputs, before, upstream, after, conv, base, skip):
    _, rows, channels = inputs.shape
    flat = pl.BlockSpec((rows, LANES), lambda i: (0, i))
    cube = pl.BlockSpec((3, rows, LANES), lambda i: (0, 0, i))
    line = pl.BlockSpec((1, LANES), lambda i: (0, i))
    return pl.pallas_call(
        mr_backward_kernel,
        grid=(channels // LANES,),
        in_specs=[
            cube, flat, flat, flat, flat,
            pl.BlockSpec((LANES // GROUP, 2 * rows), lambda i: (i, 0)),
            line,
        ],
        out_specs=[
            cube,
            pl.BlockSpec((LANES // GROUP, 8, 2 * rows), lambda i: (i, 0, 0)),
            line,
        ],
        out_shape=[
            jax.ShapeDtypeStruct((3, rows, channels), BF16),
            jax.ShapeDtypeStruct((channels // GROUP, 8, 2 * rows), F32),
            jax.ShapeDtypeStruct((1, channels), F32),
        ],
        compiler_params=pltpu.CompilerParams(vmem_limit_bytes=32 * 2**20),
        cost_estimate=pl.CostEstimate(
            flops=8 * rows * rows * channels * GROUP, bytes_accessed=24 * rows * channels,
            transcendentals=0,
        ),
        name="mr_backward",
    )(inputs, before, upstream, after, conv, base, skip)


def se_kernel(
    taps, inputs_ref, cotangent_ref, before_ref, after_ref, filter_ref, skip_ref,
    mixed_ref, grads_ref, sums_ref,
):
    rows = cotangent_ref.shape[0]
    query = inputs_ref[0].astype(F32)
    cotangent = cotangent_ref[...].astype(F32)
    key = inputs_ref[1].astype(F32)
    value = inputs_ref[2].astype(F32)
    product = (key * value).astype(BF16).astype(F32)
    gate = (cotangent * query).astype(BF16).astype(F32)
    earlier = jnp.concatenate([before_ref[...], product], 0)
    later = jnp.concatenate([gate, after_ref[...]], 0)
    pad = before_ref.shape[0]
    conv = skip_ref[...] * product
    spread = skip_ref[...] * gate
    sums = []
    for s in range(taps):
        weight = filter_ref[s : s + 1, :]
        moved = earlier[pad - s : pad - s + rows]
        conv = conv + weight * moved
        spread = spread + weight * later[s : s + rows]
        sums.append(jnp.sum(gate * moved, axis=0, keepdims=True))
    sums.append(jnp.zeros((sums_ref.shape[0] - taps, sums[0].shape[1]), F32))
    sums_ref[...] = jnp.concatenate(sums, 0)
    mixed_ref[...] = (query * conv).astype(BF16)
    grads_ref[0] = (cotangent * conv).astype(BF16)
    grads_ref[1] = (spread * value).astype(BF16)
    grads_ref[2] = (spread * key).astype(BF16)


def se_operator(inputs, cotangent, before, after, filters, skip, taps):
    _, rows, channels = inputs.shape
    halo = before.shape[0]
    flat = pl.BlockSpec((rows, LANES), lambda i: (0, i))
    cube = pl.BlockSpec((3, rows, LANES), lambda i: (0, 0, i))
    line = pl.BlockSpec((1, LANES), lambda i: (0, i))
    edge = pl.BlockSpec((halo, LANES), lambda i: (0, i))

    def kernel(*refs):
        se_kernel(taps, *refs)

    return pl.pallas_call(
        kernel,
        grid=(channels // LANES,),
        in_specs=[cube, flat, edge, edge, edge, line],
        out_specs=[flat, cube, edge],
        out_shape=[
            jax.ShapeDtypeStruct((rows, channels), BF16),
            jax.ShapeDtypeStruct((3, rows, channels), BF16),
            jax.ShapeDtypeStruct((halo, channels), F32),
        ],
        compiler_params=pltpu.CompilerParams(vmem_limit_bytes=32 * 2**20),
        cost_estimate=pl.CostEstimate(
            flops=50 * rows * channels, bytes_accessed=16 * rows * channels, transcendentals=0
        ),
        name="se_operator",
    )(inputs, cotangent, before, after, filters, skip)


MESH = pl.DeviceIdType.MESH


def greet_all(n, m, me, mine):
    barrier = pltpu.get_barrier_semaphore()

    def one(k, carry):
        there = lax.rem(me * m + mine + k, n * m)
        pl.semaphore_signal(
            barrier, inc=1, device_id=(there // m, lax.rem(there, m)), device_id_type=MESH
        )
        return carry

    lax.fori_loop(1, n * m, one, 0)
    pl.semaphore_wait(barrier, n * m - 1)


def ring_kernel(
    n, m, tile, cot_ref, weight_ref, out_ref, columns_ref, cols, sib, weight_sib, sums, outgoing,
    incoming, cot_send, cot_recv, local_sem, pair_send, pair_recv, ring_send, ring_recv,
):
    me, mine = lax.axis_index("ctx"), lax.axis_index("grp")
    rows = cot_ref.shape[0]
    channels, width = weight_ref.shape
    per = cot_ref.shape[1] // width
    half, hops = rows // 2, n // 2
    core, chip = lax.rem(me, 2), me // 2
    sibling = me + 1 - 2 * core
    depth = hops // 2

    def chip_at(place):
        turn = place // depth
        z = (1 - turn) * place + turn * (2 * depth - 1 - place)
        return 2 * z + turn

    x, z = lax.rem(chip, 2), chip // 2
    place = (1 - x) * z + x * (2 * depth - 1 - z)
    right = 2 * chip_at(lax.rem(place + 1, hops)) + core
    left = 2 * chip_at(lax.rem(place + hops - 1, hops)) + core
    greet_all(n, m, me, mine)

    def pair_copy(source, target, k):
        return pltpu.make_async_remote_copy(
            src_ref=source, dst_ref=target, send_sem=pair_send.at[k], recv_sem=pair_recv.at[k],
            device_id=(sibling, mine), device_id_type=MESH,
        )

    weight_copy = pair_copy(weight_ref, weight_sib, 0)
    weight_copy.start()

    def cot_copy(b, g, source):
        return pltpu.make_async_remote_copy(
            src_ref=cot_ref.at[:, b * width : (b + 1) * width],
            dst_ref=cols.at[lax.rem(source, 2), source // 2],
            send_sem=cot_send.at[b, g], recv_sem=cot_recv.at[source],
            device_id=(mine * per + b, g), device_id_type=MESH,
        )

    for b in range(per):
        for g in range(m):
            own = jnp.logical_and(mine * per + b == me, mine == g)

            @pl.when(jnp.logical_not(own))
            def _(b=b, g=g):
                cot_copy(b, g, me).start()

            @pl.when(own)
            def _(b=b):
                copy = pltpu.make_async_copy(
                    cot_ref.at[:, b * width : (b + 1) * width], cols.at[core, chip], local_sem
                )
                copy.start()
                copy.wait()

    def arrive(source, carry):
        own = jnp.logical_and(source == me, me // per == mine)

        @pl.when(jnp.logical_not(own))
        def _():
            cot_copy(0, 0, source).wait_recv()

        return carry

    lax.fori_loop(0, n, arrive, 0)
    cols_copy = pair_copy(cols.at[1 - core], sib, 1)
    cols_copy.start()
    columns_ref[...] = cols[...]
    weight_copy.wait_recv()
    cols_copy.wait_recv()

    def terms(owners):
        def one(t, carry):
            at = pl.ds(pl.multiple_of(t * tile, tile), tile)
            for d in range(2):
                part = pl.ds(d * half, half)
                dims = (((1,), (1,)), ((), ()))
                near = lax.dot_general(
                    cols[core, owners[d], part, :], weight_ref[at, :], dims,
                    preferred_element_type=F32,
                )
                far = lax.dot_general(
                    sib[owners[d], part, :], weight_sib[at, :], dims, preferred_element_type=F32
                )
                sums[d, :, at] = near + far
            return carry

        lax.fori_loop(0, channels // tile, one, 0)

    def hop(d, s):
        return pltpu.make_async_remote_copy(
            src_ref=outgoing.at[d, s], dst_ref=incoming.at[d, s],
            send_sem=ring_send.at[d, s], recv_sem=ring_recv.at[d, s],
            device_id=((right, left)[d], mine), device_id_type=MESH,
        )

    def owners_at(s):
        return (
            chip_at(lax.rem(place + 2 * hops - 1 - s, hops)),
            chip_at(lax.rem(place + 1 + s, hops)),
        )

    terms(owners_at(0))
    for d in range(2):
        outgoing[d, 0] = sums[d].astype(BF16)
        hop(d, 0).start()

    def step(s, carry):
        terms(owners_at(s))
        for d in range(2):
            hop(d, s - 1).wait_recv()
            outgoing[d, s] = (sums[d] + incoming[d, s - 1].astype(F32)).astype(BF16)
            hop(d, s).start()
        return carry

    lax.fori_loop(1, hops - 1, step, 0)
    terms((chip, chip))
    for d in range(2):
        hop(d, hops - 2).wait_recv()
        out_ref[d * half : (d + 1) * half] = (
            sums[d] + incoming[d, hops - 2].astype(F32)
        ).astype(BF16)

    def sent(s, carry):
        for d in range(2):
            hop(d, s).wait_send()
        return carry

    lax.fori_loop(0, hops - 1, sent, 0)
    weight_copy.wait_send()
    cols_copy.wait_send()
    for b in range(per):
        for g in range(m):
            own = jnp.logical_and(mine * per + b == me, mine == g)

            @pl.when(jnp.logical_not(own))
            def _(b=b, g=g):
                cot_copy(b, g, me).wait_send()


def ring_upstream(cotangent, weight):
    n, m = lax.axis_size("ctx"), lax.axis_size("grp")
    rows = cotangent.shape[0]
    channels, width = weight.shape
    hops, half = n // 2, rows // 2
    tile = min(1024, channels)
    dma = pltpu.SemaphoreType.DMA

    def kernel(*refs):
        ring_kernel(n, m, tile, *refs)

    vmem = pl.BlockSpec(memory_space=pltpu.VMEM)
    upstream, columns = pl.pallas_call(
        kernel,
        in_specs=[vmem, vmem],
        out_specs=[vmem, vmem],
        out_shape=[
            jax.ShapeDtypeStruct((rows, channels), BF16),
            jax.ShapeDtypeStruct((2, hops, rows, width), BF16),
        ],
        scratch_shapes=[
            pltpu.VMEM((2, hops, rows, width), BF16),
            pltpu.VMEM((hops, rows, width), BF16),
            pltpu.VMEM((channels, width), BF16),
            pltpu.VMEM((2, half, channels), F32),
            pltpu.VMEM((2, hops - 1, half, channels), BF16),
            pltpu.VMEM((2, hops - 1, half, channels), BF16),
            dma((cotangent.shape[1] // width, m)), dma((n,)), dma,
            dma((2,)), dma((2,)), dma((2, hops - 1)), dma((2, hops - 1)),
        ],
        compiler_params=pltpu.CompilerParams(
            collective_id=0, has_side_effects=True, vmem_limit_bytes=44 * 2**20
        ),
        cost_estimate=pl.CostEstimate(
            flops=2 * n * rows * channels * width, bytes_accessed=300 * 2**20, transcendentals=0
        ),
        name="ring_upstream",
    )(cotangent, weight)
    return upstream, jnp.swapaxes(columns, 0, 1).reshape(n * rows, width)


def sum_kernel(n, m, part_ref, total_ref, landed, shared, first_send, first_recv, last_send, last_recv):
    me, mine = lax.axis_index("ctx"), lax.axis_index("grp")
    barrier = pltpu.get_barrier_semaphore()

    def greet(k, carry):
        pl.semaphore_signal(
            barrier, inc=1, device_id=(lax.rem(me + k, n), mine), device_id_type=MESH
        )
        return carry

    lax.fori_loop(1, n, greet, 0)
    pl.semaphore_wait(barrier, n - 1)

    def first(k, source):
        there = lax.rem(me + k, n)
        return pltpu.make_async_remote_copy(
            src_ref=part_ref.at[there], dst_ref=landed.at[source], send_sem=first_send.at[k],
            recv_sem=first_recv.at[source], device_id=(there, mine), device_id_type=MESH,
        )

    def last(k, source):
        there = lax.rem(me + k, n)
        return pltpu.make_async_remote_copy(
            src_ref=shared.at[me], dst_ref=shared.at[source], send_sem=last_send.at[k],
            recv_sem=last_recv.at[source], device_id=(there, mine), device_id_type=MESH,
        )

    def loop(body):
        def one(k, carry):
            body(k)
            return carry

        lax.fori_loop(1, n, one, 0)

    loop(lambda k: first(k, me).start())

    def add(k, total):
        source = lax.rem(me + k, n)
        first(k, source).wait_recv()
        return total + landed[source]

    shared[me] = lax.fori_loop(1, n, add, part_ref[me])
    loop(lambda k: last(k, me).start())
    loop(lambda k: last(k, lax.rem(me + k, n)).wait_recv())
    total_ref[...] = shared[...]
    loop(lambda k: first(k, me).wait_send())
    loop(lambda k: last(k, me).wait_send())


def sum_over_ctx(part):
    n, m = lax.axis_size("ctx"), lax.axis_size("grp")
    shape = (n, part.shape[0] // n, part.shape[1])
    dma = pltpu.SemaphoreType.DMA

    def kernel(*refs):
        sum_kernel(n, m, *refs)

    vmem = pl.BlockSpec(memory_space=pltpu.VMEM)
    total = pl.pallas_call(
        kernel,
        in_specs=[vmem],
        out_specs=vmem,
        out_shape=jax.ShapeDtypeStruct(shape, F32),
        scratch_shapes=[pltpu.VMEM(shape, F32), pltpu.VMEM(shape, F32)] + [dma((n,))] * 4,
        compiler_params=pltpu.CompilerParams(
            collective_id=1, has_side_effects=True, vmem_limit_bytes=16 * 2**20
        ),
        cost_estimate=pl.CostEstimate(
            flops=part.size, bytes_accessed=40 * 2**20, transcendentals=0
        ),
        name="sum_over_ctx",
    )(part.reshape(shape))
    return total.reshape(part.shape)


def gated(left, right):
    return (left.astype(F32) * right.astype(F32)).astype(BF16)


def on_device(
    inputs_se, cotangent_se, kernel_se, skip_se, inputs_mr, kernel_mr, skip_mr, out_weight,
    cotangent_out,
):
    count = lax.axis_size("ctx")
    up = [(i, i + 1) for i in range(count - 1)]
    down = [(i + 1, i) for i in range(count - 1)]
    rows = inputs_mr.shape[1]
    channels = inputs_mr.shape[2]
    groups = channels // GROUP
    taps_se = kernel_se.shape[1]
    halo = 8

    before_mr = lax.ppermute(gated(inputs_mr[1], inputs_mr[2]), "ctx", up)
    before_se = lax.ppermute(
        gated(inputs_se[1, rows - halo :], inputs_se[2, rows - halo :]), "ctx", up
    )
    after_se = lax.ppermute(gated(cotangent_se[:halo], inputs_se[0, :halo]), "ctx", down)

    taps_f = kernel_mr.astype(F32)
    blank = jnp.zeros((groups, 1), F32)
    base_forward = jnp.concatenate(
        [blank, taps_f[:, ::-1], jnp.zeros((groups, rows - 1), F32)], 1
    )
    base_backward = jnp.concatenate([taps_f, jnp.zeros((groups, rows), F32)], 1)
    conv_mr, mixed_mr = mr_forward(inputs_mr, before_mr, base_forward, skip_mr[None])
    upstream, columns = ring_upstream(cotangent_out, out_weight)
    mixed_mr, upstream = lax.optimization_barrier((mixed_mr, upstream))
    gathered = lax.all_gather(mixed_mr, "ctx", axis=0, tiled=True)

    filters = jnp.repeat(kernel_se.astype(F32).T, GROUP, axis=1)
    filters = jnp.concatenate([filters, jnp.zeros((halo - taps_se, channels), F32)], 0)
    mixed_se, grads_se, sums_se = se_operator(
        inputs_se, cotangent_se, before_se.astype(F32), after_se.astype(F32), filters,
        skip_se[None], taps_se,
    )

    after_mr = lax.ppermute(gated(upstream, inputs_mr[0]), "ctx", down)
    grads_mr, cross, skip_part_mr = mr_backward(
        inputs_mr, before_mr, upstream, after_mr, conv_mr, base_backward, skip_mr[None]
    )
    diagonals = cross[:, 0, 1 : rows + 1]
    for b in range(1, 8):
        diagonals = diagonals + cross[:, b, b + 1 : b + rows + 1]
    kernel_part_mr = diagonals[:, ::-1]
    kernel_part_se = sums_se.reshape(halo, groups, GROUP).sum(2).T
    packed = jnp.concatenate(
        [
            kernel_part_mr,
            kernel_part_se,
            sums_se[0].reshape(groups, GROUP),
            skip_part_mr.reshape(groups, GROUP),
            jnp.zeros((groups, -(rows + halo + 2 * GROUP) % 128), F32),
        ],
        1,
    )
    packed = sum_over_ctx(packed)
    packed, gathered = lax.optimization_barrier((packed, gathered))
    at = rows + halo
    grad_kernel_mr = packed[:, :rows]
    grad_kernel_se = packed[:, rows : rows + taps_se]
    grad_skip_se = packed[:, at : at + GROUP].reshape(channels)
    grad_skip_mr = packed[:, at + GROUP : at + 2 * GROUP].reshape(channels)

    partial_value = jnp.dot(gathered, out_weight, preferred_element_type=F32).astype(BF16)
    grad_out_weight = lax.dot_general(
        gathered, columns, (((0,), (0,)), ((), ())), preferred_element_type=F32
    )
    spread_value = lax.all_to_all(partial_value, "ctx", split_axis=0, concat_axis=1, tiled=True)
    projected = lax.psum_scatter(spread_value, "grp", scatter_dimension=1, tiled=True)
    return (
        mixed_se, projected, grads_se, grads_mr, grad_kernel_se, grad_kernel_mr, grad_skip_se,
        grad_skip_mr, grad_out_weight,
    )


def solution(mesh):
    placed = (
        P(None, "ctx", "grp"),
        P("ctx", "grp"),
        P("grp", None),
        P("grp"),
        P(None, "ctx", "grp"),
        P("grp", None),
        P("grp"),
        P("grp", "ctx"),
        P("ctx", "grp"),
    )
    return jax.shard_map(
        on_device,
        mesh=mesh,
        in_specs=placed,
        out_specs=(
            P("ctx", "grp"),
            P("ctx", "grp"),
            P(None, "ctx", "grp"),
            P(None, "ctx", "grp"),
            P("grp", None),
            P("grp", None),
            P("grp"),
            P("grp"),
            P("grp", "ctx"),
        ),
        check_vma=False,
    )
```
